32 devices in a mesh: prow: 8 (over y, x, core), pcol: 4 (over z).
Axes of the slice: x: 2, y: 2, z: 4, core: 2. Of those that a mesh axis runs over, the one named last changes fastest.
Arguments:
- inverse_blocks: bfloat16 [32, 32, 128, 128], P('pcol', 'prow'), may hold values from -6 to 6
- lower_blocks: bfloat16 [32, 4, 128, 128], P('prow', None, 'pcol'), may hold values from -1 to 1
- pattern: int32 [4, 16], replicated, may hold values from 0 to 31, as said below
- diag_inverse: float32 [4, 16384], P(None, ('prow', 'pcol')), may hold values from -6 to 6
Outputs:
- inverse_column: float32 [32, 4, 128, 128], P('pcol', None, 'prow')
- inverse_diag: float32 [4, 16384], P(None, ('prow', 'pcol'))
The draws below stay inside these ranges and needn't reach their ends.
Inputs may be any that keep to these rules, and one draw needn't show every extreme that they name: `pattern`: each row names 16 different ancestor blocks.
All inputs are finite; a program needn't handle non-finite values.
Results may differ from the reference program's by a relative error of at most 0.0003.
Values may be sent and summed in bfloat16 or wider, within the bound.
No kernel may reach another device: no remote copies, remote signals or barrier semaphores. Data moves between devices by JAX's collectives and lax.ppermute only.
A program may use at most 64 MiB of HBM per device.

```python
import jax
import jax.numpy as jnp
from jax import lax

B = 128
NK = 4
G = 32
P_SIZE = 16


def draw_pattern(key, part):
    node_keys = jax.random.split(key, NK)
    picked = jax.vmap(lambda single: jax.random.permutation(single, G)[:P_SIZE])(node_keys)
    return picked.astype(jnp.int32)


def strengthened(result, rng, source, target, blocks, factor):
    def block_of(axis_at):
        return (jnp.arange(result.shape[axis_at]) // (result.shape[axis_at] // blocks)).reshape((-1,) + (1,) * (result.ndim - 1 - axis_at))

    one_side = jax.random.permutation(rng, blocks)[block_of(target)]
    other_side = (block_of(target) + blocks // 2) % blocks
    return jnp.where((block_of(source) == one_side) | (block_of(source) == other_side), factor * result, result)


def levels(own_key, extent, pieces, low, largest):
    level = 1.0
    for position, shards_of in pieces:
        steps = jax.random.uniform(jax.random.fold_in(jax.random.fold_in(own_key, 6), position), (shards_of,), jnp.float32, low / len(pieces), largest / len(pieces))
        level = level * jnp.repeat(jnp.exp(steps), extent[position] // shards_of).reshape((-1,) + (1,) * (len(extent) - 1 - position))
    return level


def bell_draw(own_key, extent, width, reach, pieces=(), kind=jnp.bfloat16):
    drawn = jax.random.normal(own_key, extent, jnp.float32) * width
    if len(pieces) > 0:
        drawn = levels(own_key, extent, pieces, -0.22, 0.18) * drawn
    return jnp.clip(drawn, min=-reach, max=reach).astype(kind)


def bell_draw_with(own_key, shape, width, most, cuts, heavy, held_as=jnp.bfloat16):
    entries = width * jax.random.normal(own_key, shape, jnp.float32)
    if cuts:
        entries = entries * levels(own_key, shape, cuts, -0.22, 0.18)
    return jnp.clip(strengthened(entries, jax.random.fold_in(own_key, 3), *heavy), -most, most).astype(held_as)


def setup_inputs(seed: int = 0) -> dict:
    keys = jax.random.split(jax.random.key(seed), 5)
    return {
        "inverse_blocks": bell_draw_with(keys[0], (G, G, B, B), ((P_SIZE * B) ** -0.15), 6.0, ((0, 4), (1, 8)), (1, 2, 8, 2.0)),
        "lower_blocks": bell_draw(keys[1], (G, NK, B, B), ((P_SIZE * B) ** -0.35), 1.0, ((0, 8), (2, 4))),
        "pattern": draw_pattern(jax.random.fold_in(keys[4], 71), 0),
        "diag_inverse": bell_draw(keys[3], (NK, B * B), 1.0, 6.0, ((1, 32),), jnp.float32),
    }


def reference(inverse_blocks, lower_blocks, pattern, diag_inverse):
    block_count = inverse_blocks.shape[0]
    node_count = lower_blocks.shape[1]
    block_width = lower_blocks.shape[3]
    matches = pattern[None, :, :] == jnp.arange(block_count, dtype=jnp.int32)[:, None, None]
    present = jnp.sum(matches.astype(jnp.float32), axis=2)
    masked = lower_blocks * present.astype(jnp.bfloat16)[:, :, None, None]
    masked_wide = masked.astype(jnp.float32)

    def one_block(packed):
        row_blocks, keep_col, own_lower = packed
        products = jnp.einsum("jrb,jkbe->kre", row_blocks.astype(jnp.float32), masked_wide, precision=lax.Precision.HIGHEST)
        column = -keep_col[:, None, None] * products
        partial_value = jnp.einsum("kra,krb->kab", own_lower, column, precision=lax.Precision.HIGHEST)
        return column, partial_value

    columns, partials = lax.map(one_block, (inverse_blocks, present, masked_wide))
    update = jnp.sum(partials, axis=0).reshape(node_count, block_width * block_width)
    return columns, diag_inverse - update
```

```python
import jax
import jax.numpy as jnp
from jax import lax
from jax.sharding import PartitionSpec as P

CORES = 2


def swap(value, axis, size, step):
    return lax.ppermute(value, axis, [(at, at ^ step) for at in range(size)])


def take(value, index, axis):
    return lax.dynamic_index_in_dim(value, index, axis, keepdims=False)


def gather_pieces(piece, axis, size):
    held = {0: piece}
    step = size // 2
    while step:
        held.update({at ^ step: swap(held[at], axis, size, step) for at in sorted(held)})
        step //= 2
    return held


def scatter_sum(parts, part_of, axis, size, own, stride):
    total = part_of(parts, own)
    for step in range(1, size):
        total = total + swap(part_of(parts, own ^ step), axis, size * stride, step * stride)
    return total


def per_device(inverse_blocks, lower_blocks, pattern, diag_inverse):
    blocks_i, blocks_j, width, _ = inverse_blocks.shape
    node_count = lower_blocks.shape[1]
    row_groups = lax.axis_size("prow")
    col_groups = lax.axis_size("pcol")
    chips = row_groups // CORES
    ratio = row_groups // col_groups
    block_count = blocks_j * row_groups
    prow, pcol = lax.axis_index("prow"), lax.axis_index("pcol")
    chip, core = prow // CORES, prow % CORES
    rows = width // row_groups

    matches = pattern[None, :, :] == jnp.arange(block_count, dtype=jnp.int32)[:, None, None]
    present = jnp.sum(matches.astype(jnp.float32), axis=2)
    keep_j = lax.dynamic_slice_in_dim(present, prow * blocks_j, blocks_j, 0)
    keep_i = lax.dynamic_slice_in_dim(present, pcol * blocks_i, blocks_i, 0)

    held = gather_pieces(lower_blocks, "pcol", col_groups)
    whole = jnp.zeros((col_groups,) + lower_blocks.shape, lower_blocks.dtype)
    for at, piece in held.items():
        whole = lax.dynamic_update_index_in_dim(whole, piece, pcol ^ at, 0)
    masked = whole * keep_j.astype(jnp.bfloat16)[None, :, :, None, None]

    by_row = lower_blocks.reshape(blocks_j, node_count, ratio, rows, width)
    own_parts = []
    for step in range(ratio):
        pairs = []
        for p in range(row_groups):
            for c in range(col_groups):
                to_p = c * ratio + (p + step) % ratio
                pairs.append((p * col_groups + c, to_p * col_groups + p // ratio))
        sent = take(by_row, (prow + step) % ratio, 2)
        own_parts.append(lax.ppermute(sent, ("prow", "pcol"), pairs))
    own = jnp.zeros((ratio,) + own_parts[0].shape, lower_blocks.dtype)
    for step, part in enumerate(own_parts):
        own = lax.dynamic_update_index_in_dim(own, part, (prow - step) % ratio, 0)
    own = own.reshape(blocks_i, node_count, rows, width) * keep_i.astype(jnp.bfloat16)[:, :, None, None]

    inv = inverse_blocks.reshape(blocks_i, blocks_j, width, col_groups, width // col_groups)
    partial_sums = jnp.einsum("ijrcb,cjkbe->rike", inv, masked, preferred_element_type=jnp.float32)
    partial_sums = partial_sums.reshape(chips, CORES, rows, blocks_i, node_count, width)
    pair_sums = take(partial_sums, core, 1) + swap(take(partial_sums, 1 - core, 1), "prow", row_groups, 1)
    summed = scatter_sum(pair_sums, lambda v, at: take(v, at, 0), "prow", chips, chip, CORES)
    column = jnp.transpose(summed, (1, 2, 0, 3)) * (-keep_i)[:, :, None, None]

    update = jnp.einsum(
        "ikra,ikrb->kab", own.astype(jnp.float32), column, precision=lax.Precision.HIGHEST
    )
    length = width * width // (row_groups * col_groups)
    update = update.reshape(node_count, chips, CORES, col_groups, length)
    update = take(update, core, 2) + swap(take(update, 1 - core, 2), "prow", row_groups, 1)
    update = scatter_sum(update, lambda v, at: take(v, at, 1), "prow", chips, chip, CORES)
    update = scatter_sum(update, lambda v, at: take(v, at, 1), "pcol", col_groups, pcol, 1)
    return column, diag_inverse - update


def solution(mesh):
    placed = (
        P("pcol", "prow", None, None),
        P("prow", None, "pcol", None),
        P(),
        P(None, ("prow", "pcol")),
    )
    return jax.shard_map(
        per_device,
        mesh=mesh,
        in_specs=placed,
        out_specs=(P("pcol", None, "prow", None), P(None, ("prow", "pcol"))),
        check_vma=False,
    )
```

```python
import jax
import jax.numpy as jnp
from jax import lax
from jax.sharding import PartitionSpec as P

CORES = 2
HEADROOM = 14.0


def swap(value, axis, size, step):
    return lax.ppermute(value, axis, [(at, at ^ step) for at in range(size)])


def take(value, index, axis):
    return lax.dynamic_index_in_dim(value, index, axis, keepdims=False)


def tied(*values):
    return lax.optimization_barrier(values)


def largest(value):
    return jnp.max(jnp.abs(value)).astype(jnp.float32)


def gather_pieces(piece, axis, size):
    held = {0: piece}
    step = size // 2
    while step:
        held.update({at ^ step: swap(held[at], axis, size, step) for at in sorted(held)})
        step //= 2
    return held


def forward(piece, at, col_groups):
    pairs = []
    for z in range(col_groups):
        for k in range(CORES):
            source, target = z * CORES + k, (z ^ at) * CORES + k
            pairs.append((source * col_groups + z, target * col_groups + z))
    return lax.ppermute(piece, ("prow", "pcol"), pairs)


def per_device(inverse_blocks, lower_blocks, pattern, diag_inverse):
    blocks_i, blocks_j, width, _ = inverse_blocks.shape
    node_count = lower_blocks.shape[1]
    row_groups = lax.axis_size("prow")
    col_groups = lax.axis_size("pcol")
    chips = row_groups // CORES
    block_count = blocks_j * row_groups
    prow, pcol = lax.axis_index("prow"), lax.axis_index("pcol")
    chip, core = prow // CORES, prow % CORES
    rows = width // row_groups

    matches = pattern[None, :, :] == jnp.arange(block_count, dtype=jnp.int32)[:, None, None]
    present = jnp.sum(matches.astype(jnp.float32), axis=2)
    keep_j = lax.dynamic_slice_in_dim(present, prow * blocks_j, blocks_j, 0)
    keep_i = lax.dynamic_slice_in_dim(present, pcol * blocks_i, blocks_i, 0)

    held = gather_pieces(lower_blocks, "pcol", col_groups)
    by_core = []
    for at in range(col_groups):
        split = held[at].reshape(blocks_j, node_count, CORES, rows, width)
        mine = take(split, core, 2)
        other = swap(take(split, 1 - core, 2), "prow", row_groups, 1)
        both = jnp.stack([jnp.where(core == 0, mine, other), jnp.where(core == 0, other, mine)])
        by_core.append(both.reshape(blocks_i, node_count, rows, width))
    own = by_core[0] * (chip == pcol).astype(lower_blocks.dtype)
    first = forward(by_core[1], 1, col_groups)

    whole = jnp.zeros((col_groups,) + lower_blocks.shape, lower_blocks.dtype)
    for at, piece in held.items():
        whole = lax.dynamic_update_index_in_dim(whole, piece, pcol ^ at, 0)
    masked = whole * keep_j.astype(jnp.bfloat16)[None, :, :, None, None]

    inv = inverse_blocks.reshape(blocks_i, blocks_j, width, col_groups, width // col_groups)
    partial_sums = jnp.einsum("ijrcb,cjkbe->rike", inv, masked, preferred_element_type=jnp.float32)
    partial_sums = partial_sums.reshape(chips, CORES, rows, blocks_i, node_count, width)
    sent, first = tied(take(partial_sums, 1 - core, 1), first)
    own = own + first
    pair_sums = take(partial_sums, core, 1) + swap(sent, "prow", row_groups, 1)
    top = jnp.max(jnp.abs(pair_sums), axis=(0, 1, 2, 3))
    power = jnp.maximum(jnp.ceil(jnp.log2(top)), -110.0)
    packed = (pair_sums * jnp.exp2(HEADROOM - power)).astype(jnp.float16).reshape(chips, -1, width)
    mark = jnp.broadcast_to(power.astype(jnp.float16), (chips, 16, width))
    packed = jnp.concatenate([packed, mark], axis=1)
    pieces = [take(packed, chip ^ step, 0) for step in range(1, chips)]
    later = by_core[2:]
    pieces, later = tied(pieces, later)
    for at in range(2, col_groups):
        own = own + forward(later[at - 2], at, col_groups)
    own = own * keep_i.astype(jnp.bfloat16)[:, :, None, None]
    summed = take(pair_sums, chip, 0)
    for step in range(1, chips):
        came = swap(pieces[step - 1], "prow", row_groups, step * CORES)
        came = lax.optimization_barrier(came.astype(jnp.float32))
        summed = summed + (came[:-16] * jnp.exp2(came[-1] - HEADROOM)).reshape(summed.shape)
    column = jnp.transpose(summed, (1, 2, 0, 3)) * (-keep_i)[:, :, None, None]

    parts = row_groups * col_groups
    wide = own.astype(jnp.float32)
    if width % parts == 0:
        update = jnp.einsum("ikra,ikrb->akb", wide, column, precision=lax.Precision.HIGHEST)
        update = update.reshape(parts, width // parts, node_count, width)
        update = jnp.sum(lax.all_to_all(update, ("prow", "pcol"), 0, 0, tiled=True), axis=0)
        update = jnp.transpose(update, (1, 0, 2)).reshape(diag_inverse.shape)
    else:
        update = jnp.einsum("ikra,ikrb->kab", wide, column, precision=lax.Precision.HIGHEST)
        update = update.reshape(node_count, parts, width * width // parts)
        update = jnp.sum(lax.all_to_all(update, ("prow", "pcol"), 1, 1, tiled=True), axis=1)
    return column, diag_inverse - update


def solution(mesh):
    placed = (
        P("pcol", "prow", None, None),
        P("prow", None, "pcol", None),
        P(),
        P(None, ("prow", "pcol")),
    )
    return jax.shard_map(
        per_device,
        mesh=mesh,
        in_specs=placed,
        out_specs=(P("pcol", None, "prow", None), P(None, ("prow", "pcol"))),
        check_vma=False,
    )
```

```python
import functools

import jax
import jax.numpy as jnp
from jax import lax
from jax.experimental import pallas as pl
from jax.experimental.pallas import tpu as pltpu
from jax.sharding import PartitionSpec as P

CORES = 2
HEADROOM = 14.0


def swap(value, axis, size, step):
    return lax.ppermute(value, axis, [(at, at ^ step) for at in range(size)])


def take(value, index, axis):
    return lax.dynamic_index_in_dim(value, index, axis, keepdims=False)


def tied(*values):
    return lax.optimization_barrier(values)


def forward(piece, bit, col_groups):
    pairs = []
    for z in range(col_groups):
        for at in range(bit):
            for k in range(CORES):
                source, target = z * CORES + k, (z ^ at ^ bit) * CORES + k
                pairs.append((source * col_groups + (z ^ at), target * col_groups + z))
    return lax.ppermute(piece, ("prow", "pcol"), pairs)


def sums_kernel(chips, rows, slices, spot_ref, keep_ref, inv_ref, met_ref, *refs):
    pieces, (out_ref, top_ref, left_ref, right_ref) = refs[: 2 * slices], refs[2 * slices :]
    blocks_i, blocks_j, width, _ = inv_ref.shape
    node_count, height = pieces[0].shape[1:3]
    depth = blocks_j * width
    core, pcol = spot_ref[0], spot_ref[1]
    for side in range(CORES):
        for at in range(slices):
            piece = pieces[side * slices + at]
            start = jnp.bitwise_xor(pcol, at) * height
            for j in range(blocks_j):
                for k in range(node_count):
                    block = jnp.where(keep_ref[side * blocks_j + j, k] > 0, piece[j, k], jnp.zeros_like(piece[j, k]))
                    row = pl.multiple_of(side * depth + j * width + start, height)
                    right_ref[pl.ds(row, height), pl.ds(k * width, width)] = block
    for q in range(chips):
        start = pl.multiple_of((q * CORES + core) * rows, rows)
        for i in range(blocks_i):
            row = pl.ds((q * blocks_i + i) * rows, rows)
            for j in range(blocks_j):
                left_ref[row, pl.ds(j * width, width)] = inv_ref[i, j, pl.ds(start, rows), :]
                left_ref[row, pl.ds(depth + j * width, width)] = met_ref[i, j, q]
    total = jnp.dot(left_ref[...], right_ref[...], preferred_element_type=jnp.float32)
    out_ref[...] = total
    top = jnp.max(jnp.abs(total), axis=0, keepdims=True)
    top_ref[...] = jnp.broadcast_to(top, top_ref.shape)


def chip_sums(spot, keep, inv, met, own_pieces, met_pieces, chips, rows):
    blocks_i, blocks_j, width, _ = inv.shape
    node_count = own_pieces[0].shape[1]
    slices = len(own_pieces)
    height = chips * blocks_i * rows
    across = node_count * width
    in_vmem = pl.BlockSpec(memory_space=pltpu.VMEM)
    in_smem = pl.BlockSpec(memory_space=pltpu.SMEM)
    depth = CORES * blocks_j * width
    return pl.pallas_call(
        functools.partial(sums_kernel, chips, rows, slices),
        out_shape=(
            jax.ShapeDtypeStruct((height, across), jnp.float32),
            jax.ShapeDtypeStruct((16, across), jnp.float32),
        ),
        in_specs=[in_smem, in_smem] + [in_vmem] * (2 + 2 * slices),
        out_specs=(in_vmem, in_vmem),
        scratch_shapes=[
            pltpu.VMEM((height, depth), jnp.bfloat16),
            pltpu.VMEM((depth, across), jnp.bfloat16),
        ],
        compiler_params=pltpu.CompilerParams(vmem_limit_bytes=24 << 20),
        cost_estimate=pl.CostEstimate(
            flops=2 * height * depth * across, bytes_accessed=4 << 20, transcendentals=0
        ),
    )(spot, keep, inv, met, *own_pieces, *met_pieces)


def plain_sums(pcol, keep, inv, met, own_pieces, met_pieces, core, chips, rows):
    blocks_i, blocks_j, width, _ = inv.shape
    node_count = own_pieces[0].shape[1]
    slices = len(own_pieces)
    mine = take(inv.reshape(blocks_i, blocks_j, chips, CORES, rows, width), core, 3)
    total = 0.0
    for side, (blocks, pieces) in enumerate(((mine, own_pieces), (met, met_pieces))):
        whole = jnp.zeros((slices,) + pieces[0].shape, pieces[0].dtype)
        for at, piece in enumerate(pieces):
            whole = lax.dynamic_update_index_in_dim(whole, piece, pcol ^ at, 0)
        shown = keep[side * blocks_j : (side + 1) * blocks_j].astype(whole.dtype)
        whole = whole * shown[:, :, None, None]
        blocks = blocks.reshape(blocks_i, blocks_j, chips, rows, slices, width // slices)
        total = total + jnp.einsum("ijqrcb,cjkbe->qirke", blocks, whole, preferred_element_type=jnp.float32)
    total = total.reshape(chips * blocks_i * rows, node_count * width)
    top = jnp.max(jnp.abs(total), axis=0, keepdims=True)
    return total, jnp.broadcast_to(top, (16, node_count * width))


def per_device(inverse_blocks, lower_blocks, pattern, diag_inverse):
    blocks_i, blocks_j, width, _ = inverse_blocks.shape
    node_count = lower_blocks.shape[1]
    row_groups = lax.axis_size("prow")
    col_groups = lax.axis_size("pcol")
    chips = row_groups // CORES
    block_count = blocks_j * row_groups
    prow, pcol = lax.axis_index("prow"), lax.axis_index("pcol")
    chip, core = prow // CORES, prow % CORES
    rows = width // row_groups
    across = node_count * width

    def core_swap(value):
        return swap(value, "prow", row_groups, 1)

    matches = pattern[None, :, :] == jnp.arange(block_count, dtype=jnp.int32)[:, None, None]
    present = jnp.sum(matches.astype(jnp.float32), axis=2)
    keep_i = lax.dynamic_slice_in_dim(present, pcol * blocks_i, blocks_i, 0)
    keep_own = lax.dynamic_slice_in_dim(present, prow * blocks_j, blocks_j, 0)
    keep_met = lax.dynamic_slice_in_dim(present, (prow ^ 1) * blocks_j, blocks_j, 0)
    keep = jnp.concatenate([keep_own, keep_met], axis=0)

    held = {0: lower_blocks}
    step = col_groups // 2
    while step:
        held.update({at ^ step: swap(held[at], "pcol", col_groups, step) for at in sorted(held)})
        step //= 2
    met_inv = core_swap(
        take(inverse_blocks.reshape(blocks_i, blocks_j, chips, CORES, rows, width), 1 - core, 3)
    )
    met = {at: core_swap(held[at]) for at in sorted(held)}

    def own_rows(at):
        cut = (blocks_j, node_count, CORES, rows, width)
        mine, other = take(held[at].reshape(cut), core, 2), take(met[at].reshape(cut), core, 2)
        both = jnp.stack([jnp.where(core == 0, mine, other), jnp.where(core == 0, other, mine)])
        return both.reshape(blocks_i, node_count, rows, width)

    bits = [1 << n for n in range(col_groups.bit_length() - 1)]
    own = own_rows(0) * (chip == pcol).astype(lower_blocks.dtype)
    first = forward(own_rows(1), 1, col_groups)
    held[col_groups - 1], first = tied(held[col_groups - 1], first)
    order = range(col_groups)
    own_pieces, met_pieces = [held[at] for at in order], [met[at] for at in order]
    if rows % 16 == 0 and (width // col_groups) % 16 == 0:
        spot = jnp.stack([core, pcol]).astype(jnp.int32)
        total, top = chip_sums(spot, keep, inverse_blocks, met_inv, own_pieces, met_pieces, chips, rows)
    else:
        total, top = plain_sums(pcol, keep, inverse_blocks, met_inv, own_pieces, met_pieces, core, chips, rows)
    power = jnp.maximum(jnp.ceil(jnp.log2(top)), -110.0)
    total = total.reshape(chips, blocks_i * rows, across)
    scaled = (total * jnp.exp2(HEADROOM - power[0])).astype(jnp.float16)
    mark = jnp.broadcast_to(power.astype(jnp.float16), (chips, 16, across))
    packed = jnp.concatenate([scaled, mark], axis=1)
    pieces = {step: take(packed, chip ^ step, 0) for step in range(1, chips)}
    own = own + first
    passed = []
    for bit in bits[1:]:
        payload, _ = tied(own_rows(bit), pieces[1])
        passed.append(forward(payload, bit, col_groups))
    summed = take(total, chip, 0)
    for step in range(1, chips):
        came = swap(pieces[step], "prow", row_groups, step * CORES)
        came = lax.optimization_barrier(came.astype(jnp.float32))
        summed = summed + came[:-16] * jnp.exp2(came[-1] - HEADROOM)
    for part in passed:
        own = own + part
    own = own * keep_i.astype(jnp.bfloat16)[:, :, None, None]
    column = summed.reshape(blocks_i, rows, node_count, width) * (-keep_i)[:, None, :, None]

    count = row_groups * col_groups
    wide = own.astype(jnp.float32)
    if width % count == 0:
        update = jnp.einsum("ikra,irkb->akb", wide, column, precision=lax.Precision.HIGHEST)
        update = update.reshape(count, width // count, node_count, width)
        update = jnp.sum(lax.all_to_all(update, ("prow", "pcol"), 0, 0, tiled=True), axis=0)
        update = jnp.transpose(update, (1, 0, 2)).reshape(diag_inverse.shape)
    else:
        update = jnp.einsum("ikra,irkb->kab", wide, column, precision=lax.Precision.HIGHEST)
        update = update.reshape(node_count, count, width * width // count)
        update = jnp.sum(lax.all_to_all(update, ("prow", "pcol"), 1, 1, tiled=True), axis=1)
    return jnp.transpose(column, (0, 2, 1, 3)), diag_inverse - update


def solution(mesh):
    placed = (
        P("pcol", "prow", None, None),
        P("prow", None, "pcol", None),
        P(),
        P(None, ("prow", "pcol")),
    )
    return jax.shard_map(
        per_device,
        mesh=mesh,
        in_specs=placed,
        out_specs=(P("pcol", None, "prow", None), P(None, ("prow", "pcol"))),
        check_vma=False,
    )
```

```python
import functools

import jax
import jax.numpy as jnp
from jax import lax
from jax.experimental import pallas as pl
from jax.experimental.pallas import tpu as pltpu
from jax.sharding import PartitionSpec as P

CORES = 2
HEADROOM = 14.0


def swap(value, axis, size, step):
    return lax.ppermute(value, axis, [(at, at ^ step) for at in range(size)])


def take(value, index, axis):
    return lax.dynamic_index_in_dim(value, index, axis, keepdims=False)


def tied(*values):
    return lax.optimization_barrier(values)


def place(right_ref, spot_ref, keep_ref, piece, side, at, blocks_j, width):
    node_count, height = piece.shape[1:3]
    start = jnp.bitwise_xor(spot_ref[1], at) * height
    for j in range(blocks_j):
        for k in range(node_count):
            block = piece[j, k]
            block = jnp.where(keep_ref[side * blocks_j + j, k] > 0, block, jnp.zeros_like(block))
            row = pl.multiple_of((side * blocks_j + j) * width + start, height)
            right_ref[pl.ds(row, height), pl.ds(k * width, width)] = block


def layout_kernel(chips, rows, spot_ref, keep_ref, inv_ref, met_ref, *refs):
    pieces, (left_ref, right_ref) = refs[:-2], refs[-2:]
    blocks_i, blocks_j, width, _ = inv_ref.shape
    half = len(pieces) // CORES
    for side in range(CORES):
        for at in range(half):
            place(right_ref, spot_ref, keep_ref, pieces[side * half + at], side, at, blocks_j, width)
    for q in range(chips):
        start = pl.multiple_of((q * CORES + spot_ref[0]) * rows, rows)
        for i in range(blocks_i):
            row = pl.ds((q * blocks_i + i) * rows, rows)
            for j in range(blocks_j):
                left_ref[row, pl.ds(j * width, width)] = inv_ref[i, j, pl.ds(start, rows), :]
                left_ref[row, pl.ds((blocks_j + j) * width, width)] = met_ref[i, j, q]


def sums_kernel(last, spot_ref, keep_ref, left_ref, given_ref, own_ref, met_ref, out_ref, top_ref, right_ref):
    blocks_j = own_ref.shape[0]
    width = own_ref.shape[3]
    right_ref[...] = given_ref[...]
    place(right_ref, spot_ref, keep_ref, own_ref, 0, last, blocks_j, width)
    place(right_ref, spot_ref, keep_ref, met_ref, 1, last, blocks_j, width)
    total = jnp.dot(left_ref[...], right_ref[...], preferred_element_type=jnp.float32)
    out_ref[...] = total
    top = jnp.max(jnp.abs(total), axis=0, keepdims=True)
    top_ref[...] = jnp.broadcast_to(top, top_ref.shape)


def laid_out(spot, keep, inv, met, own_pieces, met_pieces, chips, rows):
    blocks_i, blocks_j, width, _ = inv.shape
    node_count = own_pieces[0].shape[1]
    height, depth = chips * blocks_i * rows, CORES * blocks_j * width
    in_vmem = pl.BlockSpec(memory_space=pltpu.VMEM)
    in_smem = pl.BlockSpec(memory_space=pltpu.SMEM)
    return pl.pallas_call(
        functools.partial(layout_kernel, chips, rows),
        out_shape=(
            jax.ShapeDtypeStruct((height, depth), jnp.bfloat16),
            jax.ShapeDtypeStruct((depth, node_count * width), jnp.bfloat16),
        ),
        in_specs=[in_smem, in_smem] + [in_vmem] * (2 + 2 * len(own_pieces)),
        out_specs=(in_vmem, in_vmem),
        compiler_params=pltpu.CompilerParams(vmem_limit_bytes=24 << 20),
        cost_estimate=pl.CostEstimate(flops=0, bytes_accessed=4 << 20, transcendentals=0),
    )(spot, keep, inv, met, *own_pieces, *met_pieces)


def chip_sums(spot, keep, left, right, own_piece, met_piece, last):
    height, (depth, across) = left.shape[0], right.shape
    in_vmem = pl.BlockSpec(memory_space=pltpu.VMEM)
    in_smem = pl.BlockSpec(memory_space=pltpu.SMEM)
    return pl.pallas_call(
        functools.partial(sums_kernel, last),
        out_shape=(
            jax.ShapeDtypeStruct((height, across), jnp.float32),
            jax.ShapeDtypeStruct((16, across), jnp.float32),
        ),
        in_specs=[in_smem, in_smem] + [in_vmem] * 4,
        out_specs=(in_vmem, in_vmem),
        scratch_shapes=[pltpu.VMEM((depth, across), jnp.bfloat16)],
        compiler_params=pltpu.CompilerParams(vmem_limit_bytes=24 << 20),
        cost_estimate=pl.CostEstimate(flops=2 * height * depth * across, bytes_accessed=4 << 20, transcendentals=0),
    )(spot, keep, left, right, own_piece, met_piece)


def plain_sums(pcol, keep, inv, met, own_pieces, met_pieces, core, chips, rows):
    blocks_i, blocks_j, width, _ = inv.shape
    node_count = own_pieces[0].shape[1]
    slices = len(own_pieces)
    mine = take(inv.reshape(blocks_i, blocks_j, chips, CORES, rows, width), core, 3)
    total = 0.0
    for side, (blocks, pieces) in enumerate(((mine, own_pieces), (met, met_pieces))):
        whole = jnp.zeros((slices,) + pieces[0].shape, pieces[0].dtype)
        for at, piece in enumerate(pieces):
            whole = lax.dynamic_update_index_in_dim(whole, piece, pcol ^ at, 0)
        shown = keep[side * blocks_j : (side + 1) * blocks_j].astype(whole.dtype)
        whole = whole * shown[:, :, None, None]
        blocks = blocks.reshape(blocks_i, blocks_j, chips, rows, slices, width // slices)
        total = total + jnp.einsum("ijqrcb,cjkbe->qirke", blocks, whole, preferred_element_type=jnp.float32)
    total = total.reshape(chips * blocks_i * rows, node_count * width)
    top = jnp.max(jnp.abs(total), axis=0, keepdims=True)
    return total, jnp.broadcast_to(top, (16, node_count * width))


def per_device(inverse_blocks, lower_blocks, pattern, diag_inverse):
    blocks_i, blocks_j, width, _ = inverse_blocks.shape
    node_count = lower_blocks.shape[1]
    row_groups = lax.axis_size("prow")
    col_groups = lax.axis_size("pcol")
    chips = row_groups // CORES
    block_count = blocks_j * row_groups
    prow, pcol = lax.axis_index("prow"), lax.axis_index("pcol")
    chip, core = prow // CORES, prow % CORES
    rows = width // row_groups
    across = node_count * width

    def core_swap(value):
        return swap(value, "prow", row_groups, 1)

    matches = pattern[None, :, :] == jnp.arange(block_count, dtype=jnp.int32)[:, None, None]
    present = jnp.sum(matches.astype(jnp.float32), axis=2)
    keep_i = lax.dynamic_slice_in_dim(present, pcol * blocks_i, blocks_i, 0)
    keep_own = lax.dynamic_slice_in_dim(present, prow * blocks_j, blocks_j, 0)
    keep_met = lax.dynamic_slice_in_dim(present, (prow ^ 1) * blocks_j, blocks_j, 0)
    keep = jnp.concatenate([keep_own, keep_met], axis=0)

    held = {0: lower_blocks}
    step = col_groups // 2
    while step:
        held.update({at ^ step: swap(held[at], "pcol", col_groups, step) for at in sorted(held)})
        step //= 2
    met_inv = core_swap(
        take(inverse_blocks.reshape(blocks_i, blocks_j, chips, CORES, rows, width), 1 - core, 3)
    )
    met = {at: core_swap(held[at]) for at in sorted(held)}

    def own_rows(at):
        cut = (blocks_j, node_count, CORES, rows, width)
        mine, other = take(held[at].reshape(cut), core, 2), take(met[at].reshape(cut), core, 2)
        both = jnp.stack([jnp.where(core == 0, mine, other), jnp.where(core == 0, other, mine)])
        return both.reshape(blocks_i, node_count, rows, width)

    last = col_groups - 1
    order = range(col_groups)
    fits = rows % 16 == 0 and (width // col_groups) % 16 == 0
    spot = jnp.stack([core, pcol]).astype(jnp.int32)
    if fits:
        left, right = laid_out(
            spot, keep, inverse_blocks, met_inv,
            [held[at] for at in order[:-1]], [met[at] for at in order[:-1]], chips, rows,
        )
        held[last], left, right = tied(held[last], left, right)
        met[last] = core_swap(held[last])
    passed = {at: swap(own_rows(at), "prow", row_groups, at * CORES) for at in range(1, col_groups)}
    if fits:
        total, top = chip_sums(spot, keep, left, right, held[last], met[last], last)
    else:
        own_pieces, met_pieces = [held[at] for at in order], [met[at] for at in order]
        total, top = plain_sums(pcol, keep, inverse_blocks, met_inv, own_pieces, met_pieces, core, chips, rows)
    power = jnp.maximum(jnp.ceil(jnp.log2(top)), -110.0)
    total = total.reshape(chips, blocks_i * rows, across)
    scaled = (total * jnp.exp2(HEADROOM - power[0])).astype(jnp.float16)
    mark = jnp.broadcast_to(power.astype(jnp.float16), (chips, 16, across))
    packed = jnp.concatenate([scaled, mark], axis=1)
    pieces = {step: take(packed, chip ^ step, 0) for step in range(1, chips)}
    summed = take(total, chip, 0)
    for step in range(1, chips):
        came = swap(pieces[step], "prow", row_groups, step * CORES)
        came = lax.optimization_barrier(came.astype(jnp.float32))
        summed = summed + came[:-16] * jnp.exp2(came[-1] - HEADROOM)
    own = own_rows(0)
    for at in passed:
        own = jnp.where((chip ^ pcol) == at, passed[at], own)
    own = own * keep_i.astype(jnp.bfloat16)[:, :, None, None]
    column = summed.reshape(blocks_i, rows, node_count, width) * (-keep_i)[:, None, :, None]

    count = row_groups * col_groups
    wide = own.astype(jnp.float32)
    if width % count == 0:
        update = jnp.einsum("ikra,irkb->akb", wide, column, precision=lax.Precision.HIGHEST)
        update = update.reshape(count, width // count, node_count, width)
        update = jnp.sum(lax.all_to_all(update, ("prow", "pcol"), 0, 0, tiled=True), axis=0)
        update = jnp.transpose(update, (1, 0, 2)).reshape(diag_inverse.shape)
    else:
        update = jnp.einsum("ikra,irkb->kab", wide, column, precision=lax.Precision.HIGHEST)
        update = update.reshape(node_count, count, width * width // count)
        update = jnp.sum(lax.all_to_all(update, ("prow", "pcol"), 1, 1, tiled=True), axis=1)
    return jnp.transpose(column, (0, 2, 1, 3)), diag_inverse - update


def solution(mesh):
    placed = (
        P("pcol", "prow", None, None),
        P("prow", None, "pcol", None),
        P(),
        P(None, ("prow", "pcol")),
    )
    return jax.shard_map(
        per_device,
        mesh=mesh,
        in_specs=placed,
        out_specs=(P("pcol", None, "prow", None), P(None, ("prow", "pcol"))),
        check_vma=False,
    )
```

```python
import functools

import jax
import jax.numpy as jnp
from jax import lax
from jax.experimental import pallas as pl
from jax.experimental.pallas import tpu as pltpu
from jax.sharding import PartitionSpec as P

CORES = 2
HEADROOM = 14.0


def swap(value, axis, size, step):
    return lax.ppermute(value, axis, [(at, at ^ step) for at in range(size)])


def take(value, index, axis):
    return lax.dynamic_index_in_dim(value, index, axis, keepdims=False)


def tied(*values):
    return lax.optimization_barrier(values)


def place(right_ref, spot_ref, keep_ref, piece, side, at, blocks_j, width):
    node_count, height = piece.shape[1:3]
    start = jnp.bitwise_xor(spot_ref[1], at) * height
    for j in range(blocks_j):
        for k in range(node_count):
            block = piece[j, k]
            block = jnp.where(keep_ref[side * blocks_j + j, k] > 0, block, jnp.zeros_like(block))
            row = pl.multiple_of((side * blocks_j + j) * width + start, height)
            right_ref[pl.ds(row, height), pl.ds(k * width, width)] = block


def layout_kernel(chips, rows, spot_ref, keep_ref, inv_ref, met_ref, *refs):
    pieces, (left_ref, right_ref) = refs[:-2], refs[-2:]
    blocks_i, blocks_j, width, _ = inv_ref.shape
    half = len(pieces) // CORES
    for side in range(CORES):
        for at in range(half):
            place(right_ref, spot_ref, keep_ref, pieces[side * half + at], side, at, blocks_j, width)
    for q in range(chips):
        start = pl.multiple_of((q * CORES + spot_ref[0]) * rows, rows)
        for i in range(blocks_i):
            row = pl.ds((q * blocks_i + i) * rows, rows)
            for j in range(blocks_j):
                left_ref[row, pl.ds(j * width, width)] = inv_ref[i, j, pl.ds(start, rows), :]
                left_ref[row, pl.ds((blocks_j + j) * width, width)] = met_ref[i, j, q]


def sums_kernel(last, spot_ref, keep_ref, left_ref, given_ref, own_ref, met_ref, out_ref, top_ref, right_ref):
    blocks_j = own_ref.shape[0]
    width = own_ref.shape[3]
    right_ref[...] = given_ref[...]
    place(right_ref, spot_ref, keep_ref, own_ref, 0, last, blocks_j, width)
    place(right_ref, spot_ref, keep_ref, met_ref, 1, last, blocks_j, width)
    total = jnp.dot(left_ref[...], right_ref[...], preferred_element_type=jnp.float32)
    out_ref[...] = total
    top = jnp.max(jnp.abs(total), axis=0, keepdims=True)
    top_ref[...] = jnp.broadcast_to(top, top_ref.shape)


def laid_out(spot, keep, inv, met, own_pieces, met_pieces, chips, rows):
    blocks_i, blocks_j, width, _ = inv.shape
    node_count = own_pieces[0].shape[1]
    height, depth = chips * blocks_i * rows, CORES * blocks_j * width
    in_vmem = pl.BlockSpec(memory_space=pltpu.VMEM)
    in_smem = pl.BlockSpec(memory_space=pltpu.SMEM)
    return pl.pallas_call(
        functools.partial(layout_kernel, chips, rows),
        out_shape=(
            jax.ShapeDtypeStruct((height, depth), jnp.bfloat16),
            jax.ShapeDtypeStruct((depth, node_count * width), jnp.bfloat16),
        ),
        in_specs=[in_smem, in_smem] + [in_vmem] * (2 + 2 * len(own_pieces)),
        out_specs=(in_vmem, in_vmem),
        compiler_params=pltpu.CompilerParams(vmem_limit_bytes=24 << 20),
        cost_estimate=pl.CostEstimate(flops=0, bytes_accessed=4 << 20, transcendentals=0),
    )(spot, keep, inv, met, *own_pieces, *met_pieces)


def chip_sums(spot, keep, left, right, own_piece, met_piece, last):
    height, (depth, across) = left.shape[0], right.shape
    in_vmem = pl.BlockSpec(memory_space=pltpu.VMEM)
    in_smem = pl.BlockSpec(memory_space=pltpu.SMEM)
    return pl.pallas_call(
        functools.partial(sums_kernel, last),
        out_shape=(
            jax.ShapeDtypeStruct((height, across), jnp.float32),
            jax.ShapeDtypeStruct((16, across), jnp.float32),
        ),
        in_specs=[in_smem, in_smem] + [in_vmem] * 4,
        out_specs=(in_vmem, in_vmem),
        scratch_shapes=[pltpu.VMEM((depth, across), jnp.bfloat16)],
        compiler_params=pltpu.CompilerParams(vmem_limit_bytes=24 << 20),
        cost_estimate=pl.CostEstimate(flops=2 * height * depth * across, bytes_accessed=4 << 20, transcendentals=0),
    )(spot, keep, left, right, own_piece, met_piece)


def plain_sums(pcol, keep, inv, met, own_pieces, met_pieces, core, chips, rows):
    blocks_i, blocks_j, width, _ = inv.shape
    node_count = own_pieces[0].shape[1]
    slices = len(own_pieces)
    mine = take(inv.reshape(blocks_i, blocks_j, chips, CORES, rows, width), core, 3)
    total = 0.0
    for side, (blocks, pieces) in enumerate(((mine, own_pieces), (met, met_pieces))):
        whole = jnp.zeros((slices,) + pieces[0].shape, pieces[0].dtype)
        for at, piece in enumerate(pieces):
            whole = lax.dynamic_update_index_in_dim(whole, piece, pcol ^ at, 0)
        shown = keep[side * blocks_j : (side + 1) * blocks_j].astype(whole.dtype)
        whole = whole * shown[:, :, None, None]
        blocks = blocks.reshape(blocks_i, blocks_j, chips, rows, slices, width // slices)
        total = total + jnp.einsum("ijqrcb,cjkbe->qirke", blocks, whole, preferred_element_type=jnp.float32)
    total = total.reshape(chips * blocks_i * rows, node_count * width)
    top = jnp.max(jnp.abs(total), axis=0, keepdims=True)
    return total, jnp.broadcast_to(top, (16, node_count * width))


def per_device(inverse_blocks, lower_blocks, pattern, diag_inverse):
    blocks_i, blocks_j, width, _ = inverse_blocks.shape
    node_count = lower_blocks.shape[1]
    row_groups = lax.axis_size("prow")
    col_groups = lax.axis_size("pcol")
    chips = row_groups // CORES
    block_count = blocks_j * row_groups
    prow, pcol = lax.axis_index("prow"), lax.axis_index("pcol")
    chip, core = prow // CORES, prow % CORES
    rows = width // row_groups
    across = node_count * width

    def core_swap(value):
        return swap(value, "prow", row_groups, 1)

    matches = pattern[None, :, :] == jnp.arange(block_count, dtype=jnp.int32)[:, None, None]
    present = jnp.sum(matches.astype(jnp.float32), axis=2)
    keep_i = lax.dynamic_slice_in_dim(present, pcol * blocks_i, blocks_i, 0)
    keep_own = lax.dynamic_slice_in_dim(present, prow * blocks_j, blocks_j, 0)
    keep_met = lax.dynamic_slice_in_dim(present, (prow ^ 1) * blocks_j, blocks_j, 0)
    keep = jnp.concatenate([keep_own, keep_met], axis=0)

    held = {0: lower_blocks}
    step = col_groups // 2
    while step:
        held.update({at ^ step: swap(held[at], "pcol", col_groups, step) for at in sorted(held)})
        step //= 2
    met_inv = core_swap(
        take(inverse_blocks.reshape(blocks_i, blocks_j, chips, CORES, rows, width), 1 - core, 3)
    )
    met = {at: core_swap(held[at]) for at in sorted(held)}

    def own_rows(at):
        cut = (blocks_j, node_count, CORES, rows, width)
        mine, other = take(held[at].reshape(cut), core, 2), take(met[at].reshape(cut), core, 2)
        both = jnp.stack([jnp.where(core == 0, mine, other), jnp.where(core == 0, other, mine)])
        return both.reshape(blocks_i, node_count, rows, width)

    last = col_groups - 1
    order = range(col_groups)
    fits = rows % 16 == 0 and (width // col_groups) % 16 == 0
    spot = jnp.stack([core, pcol]).astype(jnp.int32)
    if fits:
        left, right = laid_out(
            spot, keep, inverse_blocks, met_inv,
            [held[at] for at in order[:-1]], [met[at] for at in order[:-1]], chips, rows,
        )
        held[last], left, right = tied(held[last], left, right)
        met[last] = core_swap(held[last])
    passed = {at: swap(own_rows(at), "prow", row_groups, at * CORES) for at in range(1, col_groups)}
    if fits:
        total, top = chip_sums(spot, keep, left, right, held[last], met[last], last)
    else:
        own_pieces, met_pieces = [held[at] for at in order], [met[at] for at in order]
        total, top = plain_sums(pcol, keep, inverse_blocks, met_inv, own_pieces, met_pieces, core, chips, rows)
    power = jnp.maximum(jnp.ceil(jnp.log2(top)), -110.0)
    total = total.reshape(chips, blocks_i * rows, across)
    scaled = (total * jnp.exp2(HEADROOM - power[0])).astype(jnp.float16)
    mark = jnp.broadcast_to(power[:8].astype(jnp.float16), (chips, 8, across))
    packed = jnp.concatenate([scaled, mark], axis=1)
    pieces = {step: take(packed, chip ^ step, 0) for step in range(1, chips)}
    summed = take(total, chip, 0)
    for step in range(1, chips):
        came = swap(pieces[step], "prow", row_groups, step * CORES)
        came = lax.optimization_barrier(came.astype(jnp.float32))
        summed = summed + came[:-8] * jnp.exp2(came[-1] - HEADROOM)
    own = own_rows(0)
    for at in passed:
        own = jnp.where((chip ^ pcol) == at, passed[at], own)
    own = own * keep_i.astype(jnp.bfloat16)[:, :, None, None]
    column = summed.reshape(blocks_i, rows, node_count, width) * (-keep_i)[:, None, :, None]

    count = row_groups * col_groups
    wide = own.astype(jnp.float32)
    if width % count == 0:
        update = jnp.einsum("ikra,irkb->akb", wide, column, precision=lax.Precision.HIGHEST)
        update = update.reshape(count, width // count, node_count, width)
        update = jnp.sum(lax.all_to_all(update, ("prow", "pcol"), 0, 0, tiled=True), axis=0)
        update = jnp.transpose(update, (1, 0, 2)).reshape(diag_inverse.shape)
    else:
        update = jnp.einsum("ikra,irkb->kab", wide, column, precision=lax.Precision.HIGHEST)
        update = update.reshape(node_count, count, width * width // count)
        update = jnp.sum(lax.all_to_all(update, ("prow", "pcol"), 1, 1, tiled=True), axis=1)
    return jnp.transpose(column, (0, 2, 1, 3)), diag_inverse - update


def solution(mesh):
    placed = (
        P("pcol", "prow", None, None),
        P("prow", None, "pcol", None),
        P(),
        P(None, ("prow", "pcol")),
    )
    return jax.shard_map(
        per_device,
        mesh=mesh,
        in_specs=placed,
        out_specs=(P("pcol", None, "prow", None), P(None, ("prow", "pcol"))),
        check_vma=False,
    )
```

```python
import functools

import jax
import jax.numpy as jnp
from jax import lax
from jax.experimental import pallas as pl
from jax.experimental.pallas import tpu as pltpu
from jax.sharding import PartitionSpec as P

CORES = 2
HEADROOM = 14.0


def swap(value, axis, size, step):
    return lax.ppermute(value, axis, [(at, at ^ step) for at in range(size)])


def take(value, index, axis):
    return lax.dynamic_index_in_dim(value, index, axis, keepdims=False)


def tied(*values):
    return lax.optimization_barrier(values)


def place(right_ref, spot_ref, keep_ref, piece, side, at, blocks_j, width):
    node_count, height = piece.shape[1:3]
    start = jnp.bitwise_xor(spot_ref[1], at) * height
    for j in range(blocks_j):
        for k in range(node_count):
            block = piece[j, k]
            block = jnp.where(keep_ref[side * blocks_j + j, k] > 0, block, jnp.zeros_like(block))
            row = pl.multiple_of((side * blocks_j + j) * width + start, height)
            right_ref[pl.ds(row, height), pl.ds(k * width, width)] = block


def layout_kernel(chips, rows, spot_ref, keep_ref, inv_ref, met_ref, *refs):
    pieces, (left_ref, right_ref) = refs[:-2], refs[-2:]
    blocks_i, blocks_j, width, _ = inv_ref.shape
    half = len(pieces) // CORES
    for side in range(CORES):
        for at in range(half):
            place(right_ref, spot_ref, keep_ref, pieces[side * half + at], side, at, blocks_j, width)
    for q in range(chips):
        start = pl.multiple_of((q * CORES + spot_ref[0]) * rows, rows)
        for i in range(blocks_i):
            row = pl.ds((q * blocks_i + i) * rows, rows)
            for j in range(blocks_j):
                left_ref[row, pl.ds(j * width, width)] = inv_ref[i, j, pl.ds(start, rows), :]
                left_ref[row, pl.ds((blocks_j + j) * width, width)] = met_ref[i, j, q]


def sums_kernel(last, spot_ref, keep_ref, left_ref, given_ref, own_ref, met_ref, out_ref, top_ref, right_ref):
    blocks_j = own_ref.shape[0]
    width = own_ref.shape[3]
    right_ref[...] = given_ref[...]
    place(right_ref, spot_ref, keep_ref, own_ref, 0, last, blocks_j, width)
    place(right_ref, spot_ref, keep_ref, met_ref, 1, last, blocks_j, width)
    total = jnp.dot(left_ref[...], right_ref[...], preferred_element_type=jnp.float32)
    out_ref[...] = total
    top = jnp.max(jnp.abs(total), axis=0, keepdims=True)
    top_ref[...] = jnp.broadcast_to(top, top_ref.shape)


def laid_out(spot, keep, inv, met, own_pieces, met_pieces, chips, rows):
    blocks_i, blocks_j, width, _ = inv.shape
    node_count = own_pieces[0].shape[1]
    height, depth = chips * blocks_i * rows, CORES * blocks_j * width
    in_vmem = pl.BlockSpec(memory_space=pltpu.VMEM)
    in_smem = pl.BlockSpec(memory_space=pltpu.SMEM)
    return pl.pallas_call(
        functools.partial(layout_kernel, chips, rows),
        out_shape=(
            jax.ShapeDtypeStruct((height, depth), jnp.bfloat16),
            jax.ShapeDtypeStruct((depth, node_count * width), jnp.bfloat16),
        ),
        in_specs=[in_smem, in_smem] + [in_vmem] * (2 + 2 * len(own_pieces)),
        out_specs=(in_vmem, in_vmem),
        compiler_params=pltpu.CompilerParams(vmem_limit_bytes=24 << 20),
        cost_estimate=pl.CostEstimate(flops=0, bytes_accessed=4 << 20, transcendentals=0),
    )(spot, keep, inv, met, *own_pieces, *met_pieces)


def chip_sums(spot, keep, left, right, own_piece, met_piece, last):
    height, (depth, across) = left.shape[0], right.shape
    in_vmem = pl.BlockSpec(memory_space=pltpu.VMEM)
    in_smem = pl.BlockSpec(memory_space=pltpu.SMEM)
    return pl.pallas_call(
        functools.partial(sums_kernel, last),
        out_shape=(
            jax.ShapeDtypeStruct((height, across), jnp.float32),
            jax.ShapeDtypeStruct((16, across), jnp.float32),
        ),
        in_specs=[in_smem, in_smem] + [in_vmem] * 4,
        out_specs=(in_vmem, in_vmem),
        scratch_shapes=[pltpu.VMEM((depth, across), jnp.bfloat16)],
        compiler_params=pltpu.CompilerParams(vmem_limit_bytes=24 << 20),
        cost_estimate=pl.CostEstimate(flops=2 * height * depth * across, bytes_accessed=4 << 20, transcendentals=0),
    )(spot, keep, left, right, own_piece, met_piece)


def diag_kernel(share, own_ref, sums_ref, out_ref, made_ref):
    node_count, width = own_ref.shape[1], own_ref.shape[3]
    for k in range(node_count):
        left = own_ref[:, k].reshape(sums_ref.shape[0], width)
        sums = sums_ref[:, pl.ds(k * width, width)]
        high = sums.astype(jnp.bfloat16)
        low = (sums - high.astype(jnp.float32)).astype(jnp.bfloat16)
        made = 0.0
        for part in (high, low):
            made = made + lax.dot_general(left, part, (((0,), (0,)), ((), ())), preferred_element_type=jnp.float32)
        made_ref[...] = made
        for at in range(width // share):
            out_ref[at, pl.ds(k, share, node_count), :] = made_ref[pl.ds(at * share, share), :]


def diag_pieces(own, sums, count):
    _, node_count, _, width = own.shape
    share = width // count
    in_vmem = pl.BlockSpec(memory_space=pltpu.VMEM)
    return pl.pallas_call(
        functools.partial(diag_kernel, share),
        out_shape=jax.ShapeDtypeStruct((count, node_count * share, width), jnp.float32),
        in_specs=[in_vmem, in_vmem],
        out_specs=in_vmem,
        scratch_shapes=[pltpu.VMEM((width, width), jnp.float32)],
        compiler_params=pltpu.CompilerParams(vmem_limit_bytes=24 << 20),
        cost_estimate=pl.CostEstimate(flops=4 * sums.size * width, bytes_accessed=1 << 20, transcendentals=0),
    )(own, sums)


def plain_sums(pcol, keep, inv, met, own_pieces, met_pieces, core, chips, rows):
    blocks_i, blocks_j, width, _ = inv.shape
    node_count = own_pieces[0].shape[1]
    slices = len(own_pieces)
    mine = take(inv.reshape(blocks_i, blocks_j, chips, CORES, rows, width), core, 3)
    total = 0.0
    for side, (blocks, pieces) in enumerate(((mine, own_pieces), (met, met_pieces))):
        whole = jnp.zeros((slices,) + pieces[0].shape, pieces[0].dtype)
        for at, piece in enumerate(pieces):
            whole = lax.dynamic_update_index_in_dim(whole, piece, pcol ^ at, 0)
        shown = keep[side * blocks_j : (side + 1) * blocks_j].astype(whole.dtype)
        whole = whole * shown[:, :, None, None]
        blocks = blocks.reshape(blocks_i, blocks_j, chips, rows, slices, width // slices)
        total = total + jnp.einsum("ijqrcb,cjkbe->qirke", blocks, whole, preferred_element_type=jnp.float32)
    total = total.reshape(chips * blocks_i * rows, node_count * width)
    top = jnp.max(jnp.abs(total), axis=0, keepdims=True)
    return total, jnp.broadcast_to(top, (16, node_count * width))


def per_device(inverse_blocks, lower_blocks, pattern, diag_inverse):
    blocks_i, blocks_j, width, _ = inverse_blocks.shape
    node_count = lower_blocks.shape[1]
    row_groups = lax.axis_size("prow")
    col_groups = lax.axis_size("pcol")
    chips = row_groups // CORES
    block_count = blocks_j * row_groups
    prow, pcol = lax.axis_index("prow"), lax.axis_index("pcol")
    chip, core = prow // CORES, prow % CORES
    rows = width // row_groups
    across = node_count * width

    def core_swap(value):
        return swap(value, "prow", row_groups, 1)

    matches = pattern[None, :, :] == jnp.arange(block_count, dtype=jnp.int32)[:, None, None]
    present = jnp.sum(matches.astype(jnp.float32), axis=2)
    keep_i = lax.dynamic_slice_in_dim(present, pcol * blocks_i, blocks_i, 0)
    keep_own = lax.dynamic_slice_in_dim(present, prow * blocks_j, blocks_j, 0)
    keep_met = lax.dynamic_slice_in_dim(present, (prow ^ 1) * blocks_j, blocks_j, 0)
    keep = jnp.concatenate([keep_own, keep_met], axis=0)

    held = {0: lower_blocks}
    step = col_groups // 2
    while step:
        held.update({at ^ step: swap(held[at], "pcol", col_groups, step) for at in sorted(held)})
        step //= 2
    met_inv = core_swap(
        take(inverse_blocks.reshape(blocks_i, blocks_j, chips, CORES, rows, width), 1 - core, 3)
    )
    met = {at: core_swap(held[at]) for at in sorted(held)}

    def own_rows(at):
        cut = (blocks_j, node_count, CORES, rows, width)
        mine, other = take(held[at].reshape(cut), core, 2), take(met[at].reshape(cut), core, 2)
        both = jnp.stack([jnp.where(core == 0, mine, other), jnp.where(core == 0, other, mine)])
        return both.reshape(blocks_i, node_count, rows, width)

    last = col_groups - 1
    order = range(col_groups)
    fits = rows % 16 == 0 and (width // col_groups) % 16 == 0
    spot = jnp.stack([core, pcol]).astype(jnp.int32)
    if fits:
        left, right = laid_out(
            spot, keep, inverse_blocks, met_inv,
            [held[at] for at in order[:-1]], [met[at] for at in order[:-1]], chips, rows,
        )
        held[last], left, right = tied(held[last], left, right)
        met[last] = core_swap(held[last])
    passed = {at: swap(own_rows(at), "prow", row_groups, at * CORES) for at in range(1, col_groups)}
    if fits:
        total, top = chip_sums(spot, keep, left, right, held[last], met[last], last)
    else:
        own_pieces, met_pieces = [held[at] for at in order], [met[at] for at in order]
        total, top = plain_sums(pcol, keep, inverse_blocks, met_inv, own_pieces, met_pieces, core, chips, rows)
    power = jnp.maximum(jnp.ceil(jnp.log2(top)), -110.0)
    total = total.reshape(chips, blocks_i * rows, across)
    scaled = (total * jnp.exp2(HEADROOM - power[0])).astype(jnp.float16)
    mark = jnp.broadcast_to(power[:8].astype(jnp.float16), (chips, 8, across))
    packed = jnp.concatenate([scaled, mark], axis=1)
    pieces = {step: take(packed, chip ^ step, 0) for step in range(1, chips)}
    summed = take(total, chip, 0)
    for step in range(1, chips):
        came = swap(pieces[step], "prow", row_groups, step * CORES)
        came = lax.optimization_barrier(came.astype(jnp.float32))
        summed = summed + came[:-8] * jnp.exp2(came[-1] - HEADROOM)
    own = own_rows(0)
    for at in passed:
        own = jnp.where((chip ^ pcol) == at, passed[at], own)
    own = own * keep_i.astype(jnp.bfloat16)[:, :, None, None]
    column = summed.reshape(blocks_i, rows, node_count, width) * (-keep_i)[:, None, :, None]

    count = row_groups * col_groups
    wide = own.astype(jnp.float32)
    if fits and width % count == 0:
        flipped = -diag_inverse
        summed_held, flipped = tied(summed, flipped)
        update = diag_pieces(own, summed_held, count)
        update = jnp.sum(lax.all_to_all(update, ("prow", "pcol"), 0, 0, tiled=True), axis=0)
        update = jnp.transpose(update.reshape(width // count, node_count, width), (1, 0, 2))
        return jnp.transpose(column, (0, 2, 1, 3)), update.reshape(diag_inverse.shape) - flipped
    else:
        update = jnp.einsum("ikra,irkb->kab", wide, column, precision=lax.Precision.HIGHEST)
        update = update.reshape(node_count, count, width * width // count)
        update = jnp.sum(lax.all_to_all(update, ("prow", "pcol"), 1, 1, tiled=True), axis=1)
    return jnp.transpose(column, (0, 2, 1, 3)), diag_inverse - update


def solution(mesh):
    placed = (
        P("pcol", "prow", None, None),
        P("prow", None, "pcol", None),
        P(),
        P(None, ("prow", "pcol")),
    )
    return jax.shard_map(
        per_device,
        mesh=mesh,
        in_specs=placed,
        out_specs=(P("pcol", None, "prow", None), P(None, ("prow", "pcol"))),
        check_vma=False,
    )
```

```python
import functools

import jax
import jax.numpy as jnp
from jax import lax
from jax.experimental import pallas as pl
from jax.experimental.pallas import tpu as pltpu
from jax.sharding import PartitionSpec as P

CORES = 2
HEADROOM = 14.0


def swap(value, axis, size, step):
    return lax.ppermute(value, axis, [(at, at ^ step) for at in range(size)])


def take(value, index, axis):
    return lax.dynamic_index_in_dim(value, index, axis, keepdims=False)


def tied(*values):
    return lax.optimization_barrier(values)


def place(right_ref, spot_ref, keep_ref, piece, side, at, blocks_j, width):
    node_count, height = piece.shape[1:3]
    start = jnp.bitwise_xor(spot_ref[1], at) * height
    for j in range(blocks_j):
        for k in range(node_count):
            block = piece[j, k]
            block = jnp.where(keep_ref[side * blocks_j + j, k] > 0, block, jnp.zeros_like(block))
            row = pl.multiple_of((side * blocks_j + j) * width + start, height)
            right_ref[pl.ds(row, height), pl.ds(k * width, width)] = block


def layout_kernel(chips, rows, spot_ref, keep_ref, inv_ref, met_ref, *refs):
    pieces, (left_ref, right_ref) = refs[:-2], refs[-2:]
    blocks_i, blocks_j, width, _ = inv_ref.shape
    half = len(pieces) // CORES
    for side in range(CORES):
        for at in range(half):
            place(right_ref, spot_ref, keep_ref, pieces[side * half + at], side, at, blocks_j, width)
    for q in range(chips):
        start = pl.multiple_of((q * CORES + spot_ref[0]) * rows, rows)
        for i in range(blocks_i):
            row = pl.ds((q * blocks_i + i) * rows, rows)
            for j in range(blocks_j):
                left_ref[row, pl.ds(j * width, width)] = inv_ref[i, j, pl.ds(start, rows), :]
                left_ref[row, pl.ds((blocks_j + j) * width, width)] = met_ref[i, j, q]


def sums_kernel(last, spot_ref, keep_ref, left_ref, given_ref, own_ref, met_ref, out_ref, top_ref, right_ref):
    blocks_j = own_ref.shape[0]
    width = own_ref.shape[3]
    right_ref[...] = given_ref[...]
    place(right_ref, spot_ref, keep_ref, own_ref, 0, last, blocks_j, width)
    place(right_ref, spot_ref, keep_ref, met_ref, 1, last, blocks_j, width)
    across = right_ref.shape[1] // 2
    for at in range(2):
        lanes = pl.ds(at * across, across)
        total = jnp.dot(left_ref[...], right_ref[:, lanes], preferred_element_type=jnp.float32)
        out_ref[:, lanes] = total
        top = jnp.max(jnp.abs(total), axis=0, keepdims=True)
        top_ref[:, lanes] = jnp.broadcast_to(top, (top_ref.shape[0], across))


def laid_out(spot, keep, inv, met, own_pieces, met_pieces, chips, rows):
    blocks_i, blocks_j, width, _ = inv.shape
    node_count = own_pieces[0].shape[1]
    height, depth = chips * blocks_i * rows, CORES * blocks_j * width
    in_vmem = pl.BlockSpec(memory_space=pltpu.VMEM)
    in_smem = pl.BlockSpec(memory_space=pltpu.SMEM)
    return pl.pallas_call(
        functools.partial(layout_kernel, chips, rows),
        out_shape=(
            jax.ShapeDtypeStruct((height, depth), jnp.bfloat16),
            jax.ShapeDtypeStruct((depth, node_count * width), jnp.bfloat16),
        ),
        in_specs=[in_smem, in_smem] + [in_vmem] * (2 + 2 * len(own_pieces)),
        out_specs=(in_vmem, in_vmem),
        compiler_params=pltpu.CompilerParams(vmem_limit_bytes=24 << 20),
        cost_estimate=pl.CostEstimate(flops=0, bytes_accessed=4 << 20, transcendentals=0),
    )(spot, keep, inv, met, *own_pieces, *met_pieces)


def chip_sums(spot, keep, left, right, own_piece, met_piece, last):
    height, (depth, across) = left.shape[0], right.shape
    in_vmem = pl.BlockSpec(memory_space=pltpu.VMEM)
    in_smem = pl.BlockSpec(memory_space=pltpu.SMEM)
    return pl.pallas_call(
        functools.partial(sums_kernel, last),
        out_shape=(
            jax.ShapeDtypeStruct((height, across), jnp.float32),
            jax.ShapeDtypeStruct((16, across), jnp.float32),
        ),
        in_specs=[in_smem, in_smem] + [in_vmem] * 4,
        out_specs=(in_vmem, in_vmem),
        scratch_shapes=[pltpu.VMEM((depth, across), jnp.bfloat16)],
        compiler_params=pltpu.CompilerParams(vmem_limit_bytes=24 << 20),
        cost_estimate=pl.CostEstimate(flops=2 * height * depth * across, bytes_accessed=4 << 20, transcendentals=0),
    )(spot, keep, left, right, own_piece, met_piece)


def diag_kernel(share, own_ref, sums_ref, out_ref, made_ref):
    node_count, width = own_ref.shape[1], own_ref.shape[3]
    for k in range(node_count):
        left = own_ref[:, k].reshape(sums_ref.shape[0], width)
        sums = sums_ref[:, pl.ds(k * width, width)]
        high = sums.astype(jnp.bfloat16)
        low = (sums - high.astype(jnp.float32)).astype(jnp.bfloat16)
        made = 0.0
        for part in (high, low):
            made = made + lax.dot_general(left, part, (((0,), (0,)), ((), ())), preferred_element_type=jnp.float32)
        made_ref[...] = made
        for at in range(width // share):
            out_ref[at, pl.ds(k, share, node_count), :] = made_ref[pl.ds(at * share, share), :]


def diag_pieces(own, sums, count):
    _, node_count, _, width = own.shape
    share = width // count
    in_vmem = pl.BlockSpec(memory_space=pltpu.VMEM)
    return pl.pallas_call(
        functools.partial(diag_kernel, share),
        out_shape=jax.ShapeDtypeStruct((count, node_count * share, width), jnp.float32),
        in_specs=[in_vmem, in_vmem],
        out_specs=in_vmem,
        scratch_shapes=[pltpu.VMEM((width, width), jnp.float32)],
        compiler_params=pltpu.CompilerParams(vmem_limit_bytes=24 << 20),
        cost_estimate=pl.CostEstimate(flops=4 * sums.size * width, bytes_accessed=1 << 20, transcendentals=0),
    )(own, sums)


def plain_sums(pcol, keep, inv, met, own_pieces, met_pieces, core, chips, rows):
    blocks_i, blocks_j, width, _ = inv.shape
    node_count = own_pieces[0].shape[1]
    slices = len(own_pieces)
    mine = take(inv.reshape(blocks_i, blocks_j, chips, CORES, rows, width), core, 3)
    total = 0.0
    for side, (blocks, pieces) in enumerate(((mine, own_pieces), (met, met_pieces))):
        whole = jnp.zeros((slices,) + pieces[0].shape, pieces[0].dtype)
        for at, piece in enumerate(pieces):
            whole = lax.dynamic_update_index_in_dim(whole, piece, pcol ^ at, 0)
        shown = keep[side * blocks_j : (side + 1) * blocks_j].astype(whole.dtype)
        whole = whole * shown[:, :, None, None]
        blocks = blocks.reshape(blocks_i, blocks_j, chips, rows, slices, width // slices)
        total = total + jnp.einsum("ijqrcb,cjkbe->qirke", blocks, whole, preferred_element_type=jnp.float32)
    total = total.reshape(chips * blocks_i * rows, node_count * width)
    top = jnp.max(jnp.abs(total), axis=0, keepdims=True)
    return total, jnp.broadcast_to(top, (16, node_count * width))


def per_device(inverse_blocks, lower_blocks, pattern, diag_inverse):
    blocks_i, blocks_j, width, _ = inverse_blocks.shape
    node_count = lower_blocks.shape[1]
    row_groups = lax.axis_size("prow")
    col_groups = lax.axis_size("pcol")
    chips = row_groups // CORES
    block_count = blocks_j * row_groups
    prow, pcol = lax.axis_index("prow"), lax.axis_index("pcol")
    chip, core = prow // CORES, prow % CORES
    rows = width // row_groups
    across = node_count * width

    def core_swap(value):
        return swap(value, "prow", row_groups, 1)

    matches = pattern[None, :, :] == jnp.arange(block_count, dtype=jnp.int32)[:, None, None]
    present = jnp.sum(matches.astype(jnp.float32), axis=2)
    keep_i = lax.dynamic_slice_in_dim(present, pcol * blocks_i, blocks_i, 0)
    keep_own = lax.dynamic_slice_in_dim(present, prow * blocks_j, blocks_j, 0)
    keep_met = lax.dynamic_slice_in_dim(present, (prow ^ 1) * blocks_j, blocks_j, 0)
    keep = jnp.concatenate([keep_own, keep_met], axis=0)

    held = {0: lower_blocks}
    step = col_groups // 2
    while step:
        held.update({at ^ step: swap(held[at], "pcol", col_groups, step) for at in sorted(held)})
        step //= 2
    met_inv = core_swap(
        take(inverse_blocks.reshape(blocks_i, blocks_j, chips, CORES, rows, width), 1 - core, 3)
    )
    met = {at: core_swap(held[at]) for at in sorted(held)}

    def own_rows(at):
        cut = (blocks_j, node_count, CORES, rows, width)
        mine, other = take(held[at].reshape(cut), core, 2), take(met[at].reshape(cut), core, 2)
        both = jnp.stack([jnp.where(core == 0, mine, other), jnp.where(core == 0, other, mine)])
        return both.reshape(blocks_i, node_count, rows, width)

    last = col_groups - 1
    order = range(col_groups)
    fits = rows % 16 == 0 and (width // col_groups) % 16 == 0
    spot = jnp.stack([core, pcol]).astype(jnp.int32)
    if fits:
        left, right = laid_out(
            spot, keep, inverse_blocks, met_inv,
            [held[at] for at in order[:-1]], [met[at] for at in order[:-1]], chips, rows,
        )
        held[last], left, right = tied(held[last], left, right)
        met[last] = core_swap(held[last])
    passed = {at: swap(own_rows(at), "prow", row_groups, at * CORES) for at in range(1, col_groups)}
    if fits:
        total, top = chip_sums(spot, keep, left, right, held[last], met[last], last)
    else:
        own_pieces, met_pieces = [held[at] for at in order], [met[at] for at in order]
        total, top = plain_sums(pcol, keep, inverse_blocks, met_inv, own_pieces, met_pieces, core, chips, rows)
    power = jnp.maximum(jnp.ceil(jnp.log2(top)), -110.0)
    total = total.reshape(chips, blocks_i * rows, across)
    scaled = (total * jnp.exp2(HEADROOM - power[0])).astype(jnp.float16)
    mark = jnp.broadcast_to(power[:8].astype(jnp.float16), (chips, 8, across))
    packed = jnp.concatenate([scaled, mark], axis=1)
    pieces = {step: take(packed, chip ^ step, 0) for step in range(1, chips)}
    summed = take(total, chip, 0)
    for step in range(1, chips):
        came = swap(pieces[step], "prow", row_groups, step * CORES)
        came = lax.optimization_barrier(came.astype(jnp.float32))
        summed = summed + came[:-8] * jnp.exp2(came[-1] - HEADROOM)
    own = own_rows(0)
    for at in passed:
        own = jnp.where((chip ^ pcol) == at, passed[at], own)
    own = own * keep_i.astype(jnp.bfloat16)[:, :, None, None]
    column = summed.reshape(blocks_i, rows, node_count, width) * (-keep_i)[:, None, :, None]

    count = row_groups * col_groups
    wide = own.astype(jnp.float32)
    if fits and width % count == 0:
        flipped = -diag_inverse
        summed_held, flipped = tied(summed, flipped)
        update = diag_pieces(own, summed_held, count)
        update = jnp.sum(lax.all_to_all(update, ("prow", "pcol"), 0, 0, tiled=True), axis=0)
        update = jnp.transpose(update.reshape(width // count, node_count, width), (1, 0, 2))
        return jnp.transpose(column, (0, 2, 1, 3)), update.reshape(diag_inverse.shape) - flipped
    else:
        update = jnp.einsum("ikra,irkb->kab", wide, column, precision=lax.Precision.HIGHEST)
        update = update.reshape(node_count, count, width * width // count)
        update = jnp.sum(lax.all_to_all(update, ("prow", "pcol"), 1, 1, tiled=True), axis=1)
    return jnp.transpose(column, (0, 2, 1, 3)), diag_inverse - update


def solution(mesh):
    placed = (
        P("pcol", "prow", None, None),
        P("prow", None, "pcol", None),
        P(),
        P(None, ("prow", "pcol")),
    )
    return jax.shard_map(
        per_device,
        mesh=mesh,
        in_specs=placed,
        out_specs=(P("pcol", None, "prow", None), P(None, ("prow", "pcol"))),
        check_vma=False,
    )
```
